32 devices in a mesh: grp: 2 (over x), rng: 16 (over z, y, core).
Axes of the slice: x: 2, y: 2, z: 4, core: 2. Of those that a mesh axis runs over, the one named last changes fastest.
Arguments:
- mass: bfloat16 [3072, 8, 128], P(('grp', 'rng')), parts along dimension 0, may hold values from 0.05 to 3, as said below
- classes: int32 [3072, 8], P(('grp', 'rng')), parts along dimension 0, may hold values from 0 to 15
- routes: int32 [3072, 2], P(('grp', 'rng')), parts along dimension 0, may hold values from 0 to 15, all different within a row; in each aligned block of 96 rows (0 to 95, 96 to 191, ...) at most 12 rows name the same one
- beam_weight: bfloat16 [256, 256, 1536], P(('grp', 'rng')), parts along dimension 0, may hold values from 0.0001296997 to 0.0012969971
- vertical_weight: bfloat16 [256, 256, 128], P(('grp', 'rng')), parts along dimension 0, may hold values from 0.0003828125 to 0.02890625, as said below
- ray_site: int32 [512], P('grp'), parts along dimension 0, may hold values from 0 to 7
- fit_table: float32 [16, 6], replicated, may hold values from 0.5 to 2
- site_phase: float32 [16], P('grp'), parts along dimension 0, may hold values from -1 to 1
Outputs:
- reflectivity: float32 [256, 256], P(('grp', 'rng')), parts along dimension 0
- phase: float32 [256, 256], P(('grp', 'rng')), parts along dimension 0
The draws below stay inside these ranges and needn't reach their ends.
There are 2 independent parts, one for each index of `grp`. The reference program is written for one: setup_inputs(seed, part) draws one part's arguments, and reference() takes and returns one part's arrays. A program takes and returns all parts, laid end to end along the dimension named above; an argument that names none is the same for every part. Nothing has to cross between parts.
Inputs may be any that keep to these rules, and one draw needn't show every extreme that they name: `routes`: among the rows of one device (96 aligned rows), no gate owner is named more than 12 times, and some gate owner is named exactly 12 times; the 2 entries of a row differ. Every mass content is positive. `vertical_weight`: every level weight is positive.
All inputs are finite; a program needn't handle non-finite values.
Results may differ from the reference program's by a relative error of at most 0.0004.
Values may be sent and summed in bfloat16 or wider, within the bound.
A program may use at most 64 MiB of HBM per device.

```python
import math
import jax
import jax.numpy as jnp
import numpy as np
from jax import lax

LEV = 128
COLS = 8
NTAB = 16
NSITE = 8
TOP = 2
BLK_DEV = 96
GATE_DEV = 8
RAYS = 256
BLOCKS = 1536
GATES = 128
CAP = 12
SLOTS = 192
N_RNG = 16


def level_layers(key):
    return jax.random.normal(key, (LEV,), jnp.float32)


def cell_noise(key, shape):
    return jax.random.normal(key, shape, jnp.float32)


def draw_mass(key, part):
    layers = level_layers(key)
    key = jax.random.fold_in(key, 11)
    column_key, element_key = jax.random.split(key)
    height = jnp.arange(LEV, dtype=jnp.float32) / (LEV - 1)
    column_shift = jax.random.normal(column_key, (BLOCKS, COLS, 1), jnp.float32)
    noise = cell_noise(element_key, (BLOCKS, COLS, LEV))
    level_pos = 0.9 - 0.75 * height + 0.12 * layers
    scaled = level_pos[None, None, :] + 0.08 * column_shift + 0.08 * noise
    scaled = jnp.clip(scaled, 0.0, 1.0)
    values = 0.05 * jnp.exp(math.log(60.0) * scaled)
    return values.astype(jnp.bfloat16)


def draw_vertical_weight(key, part):
    layers = level_layers(key)
    key = jax.random.fold_in(key, 23)
    elevation_key, element_key = jax.random.split(key)
    height = jnp.arange(LEV, dtype=jnp.float32) / (LEV - 1)
    elevation = jax.random.uniform(elevation_key, (1, RAYS, 1), jnp.float32, minval=0.2, maxval=0.9)
    gate_pos = (jnp.arange(GATES, dtype=jnp.float32) + 0.5) / GATES
    centre = 0.05 + elevation * gate_pos[:, None, None]
    noise = cell_noise(element_key, (GATES, RAYS, LEV))
    offset = (height[None, None, :] - centre) / 0.15
    exponent = 0.3 - 0.5 * offset * offset + 0.5 * layers[None, None, :] + 0.25 * noise
    exponent = jnp.clip(exponent, -3.0, 1.3)
    values = jnp.exp(exponent) / LEV
    return values.astype(jnp.bfloat16)


def place_ends(array, own_key, low, largest):
    extent = array.shape
    index_at = [jax.random.randint(jax.random.fold_in(own_key, axis), (), 0, extent[axis]) for axis in range(len(extent))]
    array = array.at[tuple(index_at)].set(low)
    longest = extent.index(max(extent))
    index_at[longest] = (index_at[longest] + 1) % extent[longest]
    return array.at[tuple(index_at)].set(largest)


def shard_levels(stream_key, extent, shards, low, largest):
    factor_of = 1.0
    for dim, parts in shards:
        draws = jax.random.uniform(jax.random.fold_in(jax.random.fold_in(stream_key, 6), dim), (parts,), jnp.float32, low / len(shards), largest / len(shards))
        factor_of = factor_of * jnp.repeat(jnp.exp(draws), extent[dim] // parts).reshape((-1,) + (1,) * (len(extent) - 1 - dim))
    return factor_of


def assign_block(own_key, own, number, rows, number_of, top, reach, slope):
    order = jax.random.permutation(own_key, number_of)
    heavy_load, common = shares(number_of, rows * top, reach, slope, True), shares(number_of, rows * top, reach, slope, False)
    places = jnp.arange(number_of)

    def named(lengths, turn):
        used = int((lengths > 0).sum())
        fixed = max(1, used // 4)
        passed = fixed + (places - fixed + turn * (used - fixed)) % max(1, number_of - fixed)
        return jnp.zeros((number_of,), jnp.int32).at[order[jnp.where(places < fixed, places, passed)]].set(jnp.asarray(lengths, jnp.int32))

    lengths = jnp.where(number % 4 == 0, named(heavy_load, number // 4), named(common, number - number // 4 - 1))
    mixed = jax.random.permutation(jax.random.fold_in(own, 3), number_of)
    donor, receiver = mixed[0:number_of // 2 * 2:2], mixed[1:number_of // 2 * 2:2]
    room = jnp.minimum(lengths[donor] - 1, reach - lengths[receiver]) // 2
    room = jnp.where((donor == order[0]) | (receiver == order[0]) | (lengths[receiver] == 0), 0, jnp.maximum(room, 0))
    passed = jax.random.randint(jax.random.fold_in(own, 4), (number_of // 2,), 0, 1 << 20) % (room + 1)
    lengths = lengths.at[donor].add(-passed).at[receiver].add(passed)
    items = jnp.searchsorted(jnp.cumsum(lengths), jnp.arange(rows * top), side="right").astype(jnp.int32)
    listing = items.reshape(top, rows).T
    listing = listing[jax.random.permutation(jax.random.fold_in(own, 1), rows)]
    turn = jax.random.randint(jax.random.fold_in(own, 2), (rows, 1), 0, top)
    return jnp.take_along_axis(listing, (jnp.arange(top)[None, :] + turn) % top, axis=1)


def shares(amount, total, bound, skew, full):
    loads = [(1 << 20) // math.isqrt(rank ** skew) + 1 for rank in range(1, amount + 1)]
    largest = bound if full else min(bound, max(-(-total // amount), total * loads[0] // sum(loads)))
    least = 1 if total - largest >= amount - 1 else 0
    holding, spare = [largest] + [least] * (amount - 1), total - largest - least * (amount - 1)
    while spare > 0:
        movable = [i for i in range(1, amount) if holding[i] < largest] or [i for i in range(1, amount) if holding[i] < bound]
        pool, left = sum([loads[i] for i in movable]), spare
        for i in movable:
            addition = min(bound - holding[i], max(1, left * loads[i] // pool), spare)
            holding[i] = holding[i] + addition
            spare = spare - addition
    return np.array(holding)


def setup_inputs(seed: int = 0, part: int = 0) -> dict:
    seeds = jax.random.split(jax.random.key(seed), 9)
    part_keys = jax.random.split(jax.random.fold_in(seeds[8], part), 9)
    mass = draw_mass(jax.random.fold_in(jax.random.fold_in(seeds[8], part), 71), part)
    classes = place_ends(jax.random.randint(part_keys[1], (BLOCKS, COLS), 0, NTAB), jax.random.fold_in(part_keys[1], 1), 0, NTAB - 1).astype(jnp.int32)
    routes_keys = jax.random.split(jax.random.fold_in(part_keys[2], 1), BLOCKS // BLK_DEV)
    routes_turns = jax.random.permutation(jax.random.fold_in(part_keys[2], 3), BLOCKS // BLK_DEV)
    routes = jax.vmap(lambda own, number: assign_block(jax.random.fold_in(part_keys[2], 2), own, number, BLK_DEV, N_RNG, TOP, CAP, 2))(routes_keys, routes_turns).reshape((BLOCKS, TOP))
    beam_weight = jnp.clip(jnp.exp(math.log(0.0012969971) - 2.3025851 * jax.random.uniform(part_keys[3], (GATES, RAYS, SLOTS * COLS), jnp.float32) ** shard_levels(part_keys[3], (GATES, RAYS, SLOTS * COLS), ((0, 16),), -0.2, 0.2)), 0.0001296997, 0.0012969971).astype(jnp.bfloat16)
    vertical_weight = draw_vertical_weight(jax.random.fold_in(jax.random.fold_in(seeds[8], part), 71), part)
    ray_site = place_ends(jax.random.randint(part_keys[5], (RAYS,), 0, NSITE), jax.random.fold_in(part_keys[5], 1), 0, NSITE - 1).astype(jnp.int32)
    fit_table = jnp.clip(jax.random.uniform(seeds[6], (NTAB, 6), jnp.float32, 0.5, 2.0), 0.5, 2.0)
    site_phase = jnp.clip(jax.random.uniform(part_keys[7], (NSITE,), jnp.float32, -1.0, 1.0), -1.0, 1.0)
    return dict(mass=mass, classes=classes, routes=routes, beam_weight=beam_weight, vertical_weight=vertical_weight, ray_site=ray_site, fit_table=fit_table, site_phase=site_phase)


def scatter_fit(mass_values, class_onehot, fit_table):
    coeffs = jnp.sum(class_onehot[..., None] * fit_table, axis=-2)
    positive = mass_values > 0
    safe_mass = jnp.where(positive, mass_values, 1.0)
    log_mass = jnp.log(safe_mass)[..., None, :]
    prefactor = coeffs[..., 0::2][..., None]
    exponent = coeffs[..., 1::2][..., None]
    channels = prefactor * jnp.exp(exponent * log_mass)
    channels = jnp.where(positive[..., None, :], channels, 0.0)
    return channels.reshape(channels.shape[:-2] + (3 * channels.shape[-1],))


def reference(mass, classes, routes, beam_weight, vertical_weight, ray_site, fit_table, site_phase):
    class_onehot = (classes[..., None] == jnp.arange(NTAB, dtype=jnp.int32)).astype(jnp.float32)
    fields = scatter_fit(mass.astype(jnp.float32), class_onehot, fit_table).astype(jnp.bfloat16)
    pair_count = BLK_DEV * TOP
    targets = routes.reshape(N_RNG, pair_count).astype(jnp.int32)
    target_hot = (targets[..., None] == jnp.arange(N_RNG, dtype=jnp.int32)).astype(jnp.int32)
    position = jnp.sum((jnp.cumsum(target_hot, axis=1) - target_hot) * target_hot, axis=-1).astype(jnp.int32)
    sources = jnp.broadcast_to(jnp.arange(N_RNG, dtype=jnp.int32)[:, None], targets.shape)
    block_ids = (jnp.arange(N_RNG * pair_count, dtype=jnp.int32) // TOP).reshape(N_RNG, pair_count)
    inverse = jnp.full((N_RNG, SLOTS), -1, jnp.int32).at[targets, sources * CAP + position].set(block_ids)
    cells = GATE_DEV * RAYS

    def owner_beam(operands):
        slot_ids, weights, vertical = operands
        valid = slot_ids >= 0
        picked = fields[jnp.maximum(slot_ids, 0).astype(jnp.int32)]
        picked = jnp.where(valid[:, None, None], picked, jnp.zeros_like(picked))
        received = picked.reshape(SLOTS * COLS, 3 * LEV)
        sampled = jnp.dot(weights, received, preferred_element_type=jnp.float32)
        sampled = sampled.reshape(cells, 3, LEV)
        return jnp.sum(sampled * vertical.astype(jnp.float32)[:, None, :], axis=-1)

    beams = lax.map(owner_beam, (inverse, beam_weight.reshape(N_RNG, cells, SLOTS * COLS), vertical_weight.reshape(N_RNG, cells, LEV)))
    beams = beams.reshape(GATES, RAYS, 3)
    refl_lin = beams[..., 0]
    atten = beams[..., 1]
    spec_phase = beams[..., 2]
    step_len = 4.0 / GATES
    depth = step_len * (jnp.cumsum(atten, axis=0) - 0.5 * atten)
    reflectivity = jnp.log(refl_lin) - 2.0 * depth
    offsets = jnp.sum((ray_site[:, None] == jnp.arange(NSITE, dtype=jnp.int32)[None, :]).astype(jnp.float32) * site_phase[None, :], axis=1)
    phase = 2.0 * step_len * jnp.cumsum(spec_phase, axis=0) + offsets[None, :]
    return reflectivity, phase
```

```python
import functools

import jax
import jax.numpy as jnp
from jax import lax
from jax.experimental import pallas as pl
from jax.experimental.pallas import tpu as pltpu
from jax.sharding import PartitionSpec as P

MESH = pl.DeviceIdType.MESH
BF16, F32 = jnp.bfloat16, jnp.float32
PLANES = 4


def iota(shape, dim):
    return lax.broadcasted_iota(jnp.int32, shape, dim)


def block_of(index, size):
    return jnp.floor((index.astype(F32) + 0.5) * (1.0 / size))


def dot(a, b, contract=((1,), (0,)), precision=None):
    return lax.dot_general(
        a, b, (contract, ((), ())), preferred_element_type=F32, precision=precision
    )


def kernel(
    n, cap,
    mass_ref, classes_ref, routes_ref, ray_ref, table_ref, site_ref, weight_hbm, vertical_hbm,
    refl_ref, phase_ref,
    weight, vertical, vertical_t, mass_f32, slots_f32, out_mass, out_class, in_mass, in_class,
    out_total, in_total, beam_acc, load_sem, send_sem, recv_sem,
):
    me = lax.axis_index("rng")
    blocks, cols, levels = mass_ref.shape
    gates, rays = refl_ref.shape
    members = n // PLANES
    chunk = cap * cols
    depth = members * chunk
    slots = n * cap
    plane, place = me // members, me % members
    half = plane // 2

    def to(rank):
        return {"rng": rank}

    barrier = pltpu.get_barrier_semaphore()

    def greet(i, _):
        pl.semaphore_signal(barrier, 1, device_id=to((me + i) % n), device_id_type=MESH)
        return 0

    lax.fori_loop(1, n, greet, 0)

    def weight_load(z):
        return pltpu.make_async_copy(
            weight_hbm.at[:, pl.ds(z * depth, depth)], weight.at[z], load_sem.at[z]
        )

    vertical_load = pltpu.make_async_copy(vertical_hbm, vertical, load_sem.at[PLANES])
    vertical_load.start()
    for z in range(PLANES):
        weight_load(z).start()

    owner = iota((blocks, n), 1)
    named = (routes_ref[:, 0:1] == owner) | (routes_ref[:, 1:2] == owner)
    earlier = (iota((blocks, blocks), 1) < iota((blocks, blocks), 0)).astype(F32).astype(BF16)
    position = dot(earlier, named.astype(F32).astype(BF16))
    position = jnp.where(named, position, -1.0).astype(BF16)
    slot_lane = iota((n, slots), 1)
    first = iota((n, slots), 0) * cap
    spread = ((slot_lane >= first) & (slot_lane < first + cap)).astype(F32).astype(BF16)
    lane = iota((blocks, slots), 1)
    lane_position = lane.astype(F32) - cap * block_of(lane, cap)
    fills = (dot(position, spread) == lane_position).astype(F32).astype(BF16)

    mass_f32[...] = mass_ref[...].astype(F32).reshape(blocks * cols, levels)
    by_block = jnp.concatenate(
        [mass_f32[pl.ds(c, blocks, stride=cols), :].astype(BF16) for c in range(cols)], axis=1
    )
    picked = dot(fills, by_block, ((0,), (0,)))
    for c in range(cols):
        slots_f32[pl.ds(c, slots, stride=cols), :] = picked[:, c * levels : (c + 1) * levels]
    out_mass[...] = slots_f32[...].astype(BF16).reshape(n, chunk, levels)

    tile = iota((cols, 128), 1)
    tile_col = tile.astype(F32) - cols * block_of(tile, cols)
    tile = (tile_col == iota((cols, 128), 0).astype(F32)).astype(F32).astype(BF16)
    class_tiles = dot(classes_ref[...].astype(F32).astype(BF16), tile).astype(BF16)
    slot_class = dot(fills, class_tiles, ((0,), (0,)))
    row = iota((slots, 128), 0)
    row_position = row.astype(F32) - cap * block_of(row, cap)
    own_lanes = block_of(iota((slots, 128), 1), cols) == row_position
    class_rows = dot(spread, jnp.where(own_lanes, slot_class, 0.0).astype(BF16))
    out_class[...] = class_rows.reshape(n, 1, 128)

    def mass_copy(target, source):
        return pltpu.make_async_remote_copy(
            src_ref=out_mass.at[target], dst_ref=in_mass.at[source],
            send_sem=send_sem.at[0, target], recv_sem=recv_sem.at[0, source],
            device_id=to(target), device_id_type=MESH,
        )

    def class_copy(target, source):
        return pltpu.make_async_remote_copy(
            src_ref=out_class.at[target], dst_ref=in_class.at[source],
            send_sem=send_sem.at[1, target], recv_sem=recv_sem.at[1, source],
            device_id=to(target), device_id_type=MESH,
        )

    def total_copy(target, source):
        return pltpu.make_async_remote_copy(
            src_ref=out_total, dst_ref=in_total.at[source],
            send_sem=send_sem.at[2, target], recv_sem=recv_sem.at[2, source],
            device_id=to(target), device_id_type=MESH,
        )

    near = plane + 1 - 2 * (plane % 2)
    far, farthest = 2 - half, 3 - 3 * half

    def each(z, start, act):
        def step(i, _):
            act(z * members + (place + i) % members)
            return 0

        lax.fori_loop(start, members, step, 0)

    def send(target):
        class_copy(target, me).start()
        mass_copy(target, me).start()

    def arrive(source):
        class_copy(source, source).wait_recv()
        mass_copy(source, source).wait_recv()

    pl.semaphore_wait(barrier, n - 1)
    each(farthest, 0, send)
    each(far, 0, send)
    each(near, 0, send)
    each(plane, 1, send)

    in_mass[me] = out_mass[me]
    in_class[me] = out_class[me]

    vertical_load.wait()
    vertical_t[...] = vertical[...].astype(F32).T
    for z in range(PLANES):
        weight_load(z).wait()

    lane = iota((chunk, depth), 1)
    lane_place = block_of(lane, chunk)
    unroll = (lane.astype(F32) - chunk * lane_place == iota((chunk, depth), 0).astype(F32))
    unroll = unroll.astype(F32).astype(BF16)
    from_place = block_of(iota((members, depth), 1), chunk) == iota((members, depth), 0).astype(F32)

    def absorb(z, initial):
        chosen = pl.ds(z * members, members)
        class_grid = in_class[chosen].reshape(members, 128)[:, :chunk].astype(BF16)
        class_row = jnp.sum(jnp.where(from_place, dot(class_grid, unroll), 0.0), axis=0, keepdims=True)
        onehot = (class_row == iota((table_ref.shape[0], depth), 0).astype(F32)).astype(F32)
        coeffs = dot(table_ref[...], onehot, ((0,), (0,)), lax.Precision.HIGHEST)
        mass_t = in_mass[chosen].reshape(depth, levels).astype(F32).T
        positive = mass_t > 0
        log_mass = jnp.log2(jnp.where(positive, mass_t, 1.0))
        fields_t = jnp.concatenate(
            [
                jnp.where(
                    positive,
                    coeffs[2 * j : 2 * j + 1] * jnp.exp2(coeffs[2 * j + 1 : 2 * j + 2] * log_mass),
                    0.0,
                ).astype(BF16)
                for j in range(3)
            ],
            axis=0,
        )
        for g in range(gates):
            cells = slice(g * rays, (g + 1) * rays)
            sampled = dot(fields_t, weight[z, cells, :], ((1,), (1,)))
            v = vertical_t[:, cells]
            for j in range(3):
                part = sampled[j * levels : (j + 1) * levels] * v
                part = jnp.sum(part.reshape(levels // 8, 8, rays), axis=0)
                if initial:
                    beam_acc[j, :, cells] = part
                else:
                    beam_acc[j, :, cells] += part

    each(plane, 1, arrive)
    absorb(plane, True)
    each(near, 0, arrive)
    absorb(near, False)
    each(far, 0, arrive)
    absorb(far, False)
    each(farthest, 0, arrive)
    absorb(farthest, False)

    gate_row = iota((gates, rays), 0)

    def gate_rows(j):
        rows = jnp.zeros((gates, rays), F32)
        for g in range(gates):
            beam = jnp.sum(beam_acc[j, :, g * rays : (g + 1) * rays], axis=0, keepdims=True)
            rows = jnp.where(gate_row == g, beam, rows)
        return rows

    atten, spec_phase = gate_rows(1), gate_rows(2)
    out_total[0:1, :] = jnp.sum(atten, axis=0, keepdims=True)
    out_total[1:2, :] = jnp.sum(spec_phase, axis=0, keepdims=True)

    def send_total(target):
        total_copy(target, me).start()

    for z, start in ((farthest, 0), (far, 0), (near, 0), (plane, 1)):
        each(z, start, send_total)

    def running(rows):
        sums = jnp.zeros((gates, rays), F32)
        for g in range(gates):
            sums = sums + jnp.where(gate_row >= g, rows[g : g + 1], 0.0)
        return sums

    log_refl = jnp.log(gate_rows(0))
    atten_depth = running(atten) - 0.5 * atten
    phase_sum = running(spec_phase)
    offsets = jnp.zeros((1, rays), F32)
    for i in range(site_ref.shape[1]):
        offsets = offsets + jnp.where(ray_ref[...] == i, site_ref[0, i], 0.0)

    for z, start in ((plane, 1), (near, 0), (far, 0), (farthest, 0)):
        each(z, start, lambda source: total_copy(source, source).wait_recv())

    in_total[me] = out_total[...]
    sources = in_total[...]
    before = jnp.sum(jnp.where(iota(sources.shape, 0) < me, sources, 0.0), axis=0)
    step_len = 4.0 / (n * gates)
    refl_ref[...] = log_refl - 2.0 * step_len * (before[0:1] + atten_depth)
    phase_ref[...] = 2.0 * step_len * (before[1:2] + phase_sum) + offsets

    def sent(target):
        class_copy(target, me).wait_send()
        mass_copy(target, me).wait_send()
        total_copy(target, me).wait_send()

    for z, start in ((plane, 1), (near, 0), (far, 0), (farthest, 0)):
        each(z, start, sent)


def local(mass, classes, routes, beam_weight, vertical_weight, ray_site, fit_table, site_phase):
    n = lax.axis_size("rng")
    blocks, cols, levels = mass.shape
    gates, rays, slot_cols = beam_weight.shape
    cap = slot_cols // (n * cols)
    cells = gates * rays
    chunk = cap * cols
    vmem, hbm = pl.BlockSpec(memory_space=pltpu.VMEM), pl.BlockSpec(memory_space=pl.ANY)
    smem = pl.BlockSpec(memory_space=pltpu.SMEM)
    return pl.pallas_call(
        functools.partial(kernel, n, cap),
        out_shape=(jax.ShapeDtypeStruct((gates, rays), F32),) * 2,
        in_specs=[vmem, vmem, vmem, vmem, vmem, smem, hbm, hbm],
        out_specs=(vmem, vmem),
        scratch_shapes=[
            pltpu.VMEM((PLANES, cells, slot_cols // PLANES), BF16),
            pltpu.VMEM((cells, levels), BF16),
            pltpu.VMEM((levels, cells), F32),
            pltpu.VMEM((blocks * cols, levels), F32),
            pltpu.VMEM((slot_cols, levels), F32),
            pltpu.VMEM((n, chunk, levels), BF16),
            pltpu.VMEM((n, 1, 128), F32),
            pltpu.VMEM((n, chunk, levels), BF16),
            pltpu.VMEM((n, 1, 128), F32),
            pltpu.VMEM((2, rays), F32),
            pltpu.VMEM((n, 2, rays), F32),
            pltpu.VMEM((3, 8, cells), F32),
            pltpu.SemaphoreType.DMA((PLANES + 1,)),
            pltpu.SemaphoreType.DMA((3, n)),
            pltpu.SemaphoreType.DMA((3, n)),
        ],
        compiler_params=pltpu.CompilerParams(
            collective_id=0, has_side_effects=True, vmem_limit_bytes=56 * 1024 * 1024
        ),
    )(
        mass, classes, routes, ray_site.reshape(1, rays), fit_table, site_phase.reshape(1, -1),
        beam_weight.reshape(cells, slot_cols), vertical_weight.reshape(cells, levels),
    )


def solution(mesh):
    placed = (
        P(("grp", "rng"), None, None),
        P(("grp", "rng"), None),
        P(("grp", "rng"), None),
        P(("grp", "rng"), None, None),
        P(("grp", "rng"), None, None),
        P("grp"),
        P(),
        P("grp"),
    )
    return jax.shard_map(
        local,
        mesh=mesh,
        in_specs=placed,
        out_specs=(P(("grp", "rng"), None), P(("grp", "rng"), None)),
        check_vma=False,
    )
```

```python
import functools

import jax
import jax.numpy as jnp
from jax import lax
from jax.experimental import pallas as pl
from jax.experimental.pallas import tpu as pltpu
from jax.sharding import PartitionSpec as P

MESH = pl.DeviceIdType.MESH
BF16, F32 = jnp.bfloat16, jnp.float32
PLANES = 4


def iota(shape, dim):
    return lax.broadcasted_iota(jnp.int32, shape, dim)


def block_of(index, size):
    return jnp.floor((index.astype(F32) + 0.5) * (1.0 / size))


def dot(a, b, contract=((1,), (0,)), precision=None):
    return lax.dot_general(
        a, b, (contract, ((), ())), preferred_element_type=F32, precision=precision
    )


def kernel(
    n, cap,
    mass_hbm, classes_hbm, routes_hbm, ray_hbm, table_hbm, site_hbm, weight_hbm, vertical_hbm,
    refl_ref, phase_ref,
    mass_ref, classes_ref, routes_ref, ray_ref, table_ref, site_ref,
    weight, vertical, vertical_t, mass_f32, slots_f32, out_mass, out_class, in_mass, in_class,
    out_total, in_total, beam_acc, load_sem, send_sem, mass_sem, class_sem, total_sem,
):
    me = lax.axis_index("rng")
    blocks, cols, levels = mass_ref.shape
    gates, rays = refl_ref.shape
    members = n // PLANES
    chunk = cap * cols
    depth = members * chunk
    slots = n * cap
    plane, place = me // members, me % members
    half = plane // 2

    def to(rank):
        return {"rng": rank}

    barrier = pltpu.get_barrier_semaphore()

    def greet(i, _):
        pl.semaphore_signal(barrier, 1, device_id=to((me + i) % n), device_id_type=MESH)
        return 0

    lax.fori_loop(1, n, greet, 0, unroll=n <= 16)

    small = [
        pltpu.make_async_copy(source, target, load_sem.at[PLANES + 1 + i])
        for i, (source, target) in enumerate(
            (
                (routes_hbm, routes_ref),
                (mass_hbm, mass_ref),
                (classes_hbm, classes_ref),
                (table_hbm, table_ref),
                (ray_hbm, ray_ref),
                (site_hbm, site_ref),
            )
        )
    ]
    for copy in small:
        copy.start()

    def weight_load(z):
        return pltpu.make_async_copy(
            weight_hbm.at[:, pl.ds(z * depth, depth)], weight.at[z], load_sem.at[z]
        )

    vertical_load = pltpu.make_async_copy(vertical_hbm, vertical, load_sem.at[PLANES])
    vertical_load.start()
    for z in range(PLANES):
        weight_load(z).start()

    for copy in small[:3]:
        copy.wait()

    owner = iota((n, blocks), 0)
    named = (routes_ref[0:1, :] == owner) | (routes_ref[1:2, :] == owner)
    earlier = (iota((blocks, blocks), 0) < iota((blocks, blocks), 1)).astype(F32).astype(BF16)
    position = dot(named.astype(F32).astype(BF16), earlier)
    position = jnp.where(named, position, -1.0).astype(BF16)
    row = iota((slots, n), 0).astype(F32)
    owns = (block_of(row, cap) == iota((slots, n), 1).astype(F32)).astype(F32).astype(BF16)
    row = iota((slots, blocks), 0).astype(F32)
    fills = (dot(owns, position) == row - cap * block_of(row, cap)).astype(F32).astype(BF16)

    mass_f32[...] = mass_ref[...].astype(F32).reshape(blocks * cols, levels)
    by_block = jnp.concatenate(
        [mass_f32[pl.ds(c, blocks, stride=cols), :].astype(BF16) for c in range(cols)], axis=1
    )
    picked = dot(fills, by_block)
    for c in range(cols):
        slots_f32[pl.ds(c, slots, stride=cols), :] = picked[:, c * levels : (c + 1) * levels]
    out_mass[...] = slots_f32[...].astype(BF16).reshape(n, chunk, levels)

    slot_class = dot(fills, classes_ref[...].astype(F32).astype(BF16), ((1,), (1,))).astype(BF16)
    tile = iota((cols, 128), 1).astype(F32)
    tile = tile - cols * block_of(tile, cols) == iota((cols, 128), 0).astype(F32)
    row = iota((slots, 128), 0).astype(F32)
    own_lanes = block_of(iota((slots, 128), 1), cols) == row - cap * block_of(row, cap)
    tiled = jnp.where(own_lanes, dot(slot_class, tile.astype(F32).astype(BF16)), 0.0).astype(BF16)
    spread = (block_of(iota((n, slots), 1), cap) == iota((n, slots), 0).astype(F32))
    class_rows = dot(spread.astype(F32).astype(BF16), tiled)
    out_class[...] = class_rows.reshape(n, 1, 128)

    def mass_copy(target):
        return pltpu.make_async_remote_copy(
            src_ref=out_mass.at[target], dst_ref=in_mass.at[me],
            send_sem=send_sem.at[0], recv_sem=mass_sem.at[plane],
            device_id=to(target), device_id_type=MESH,
        )

    def class_copy(target):
        return pltpu.make_async_remote_copy(
            src_ref=out_class.at[target], dst_ref=in_class.at[me],
            send_sem=send_sem.at[1], recv_sem=class_sem.at[plane],
            device_id=to(target), device_id_type=MESH,
        )

    def total_copy(target):
        return pltpu.make_async_remote_copy(
            src_ref=out_total, dst_ref=in_total.at[me],
            send_sem=send_sem.at[2], recv_sem=total_sem,
            device_id=to(target), device_id_type=MESH,
        )

    def wait_bytes(ref, count, sem):
        part = ref.at[pl.ds(0, count)]
        pltpu.make_async_copy(part, part, sem).wait()

    near = plane + 1 - 2 * (plane % 2)
    far, last = (plane + 2) % PLANES, PLANES - 1 - plane
    others = ((last, 0), (far, 0), (near, 0), (plane, 1))

    def each(z, start, act):
        def step(i, _):
            act(z * members + (place + i) % members)
            return 0

        lax.fori_loop(start, members, step, 0, unroll=n <= 16)

    def arrive(z, count):
        wait_bytes(in_class, count, class_sem.at[z])
        wait_bytes(in_mass, count, mass_sem.at[z])

    pl.semaphore_wait(barrier, n - 1)
    for z, start in ((far, 0), (last, 0), (near, 0), (plane, 1)):
        each(z, start, lambda target: mass_copy(target).start())
        each(z, start, lambda target: class_copy(target).start())

    in_mass[me] = out_mass[me]
    in_class[me] = out_class[me]

    for copy in small[3:]:
        copy.wait()
    vertical_load.wait()
    vertical_t[...] = vertical[...].astype(F32).T
    for z in range(PLANES):
        weight_load(z).wait()

    lane = iota((chunk, depth), 1)
    lane_place = block_of(lane, chunk)
    unroll = (lane.astype(F32) - chunk * lane_place == iota((chunk, depth), 0).astype(F32))
    unroll = unroll.astype(F32).astype(BF16)
    from_place = block_of(iota((members, depth), 1), chunk) == iota((members, depth), 0).astype(F32)

    def absorb(z, initial):
        chosen = pl.ds(z * members, members)
        class_grid = in_class[chosen].reshape(members, 128)[:, :chunk].astype(BF16)
        class_row = jnp.sum(jnp.where(from_place, dot(class_grid, unroll), 0.0), axis=0, keepdims=True)
        onehot = (class_row == iota((table_ref.shape[1], depth), 0).astype(F32)).astype(F32)
        coeffs = dot(table_ref[...], onehot, precision=lax.Precision.HIGHEST)
        mass_t = in_mass[chosen].reshape(depth, levels).astype(F32).T
        positive = mass_t > 0
        log_mass = jnp.log2(jnp.where(positive, mass_t, 1.0))
        fields_t = jnp.concatenate(
            [
                jnp.where(
                    positive,
                    coeffs[2 * j : 2 * j + 1] * jnp.exp2(coeffs[2 * j + 1 : 2 * j + 2] * log_mass),
                    0.0,
                ).astype(BF16)
                for j in range(3)
            ],
            axis=0,
        )
        for g in range(gates):
            cells = slice(g * rays, (g + 1) * rays)
            sampled = dot(fields_t, weight[z, cells, :], ((1,), (1,)))
            v = vertical_t[:, cells]
            for j in range(3):
                part = sampled[j * levels : (j + 1) * levels] * v
                part = jnp.sum(part.reshape(levels // 8, 8, rays), axis=0)
                if initial:
                    beam_acc[j, :, cells] = part
                else:
                    beam_acc[j, :, cells] += part

    arrive(plane, members - 1)
    absorb(plane, True)
    for z in (near, far, last):
        arrive(z, members)
        absorb(z, False)

    gate_row = iota((gates, rays), 0)

    def gate_rows(j):
        rows = jnp.zeros((gates, rays), F32)
        for g in range(gates):
            beam = jnp.sum(beam_acc[j, :, g * rays : (g + 1) * rays], axis=0, keepdims=True)
            rows = jnp.where(gate_row == g, beam, rows)
        return rows

    for j in range(2):
        sums = beam_acc[j + 1, :, 0:rays]
        for g in range(1, gates):
            sums = sums + beam_acc[j + 1, :, g * rays : (g + 1) * rays]
        out_total[j : j + 1, :] = jnp.sum(sums, axis=0, keepdims=True)
    for z, start in others:
        each(z, start, lambda target: total_copy(target).start())

    atten, spec_phase = gate_rows(1), gate_rows(2)
    in_total[me] = out_total[...]
    wait_bytes(out_mass, n - 1, send_sem.at[0])
    wait_bytes(out_class, n - 1, send_sem.at[1])

    def running(rows):
        sums = jnp.zeros((gates, rays), F32)
        for g in range(gates):
            sums = sums + jnp.where(gate_row >= g, rows[g : g + 1], 0.0)
        return sums

    log_refl = jnp.log(gate_rows(0))
    atten_depth = running(atten) - 0.5 * atten
    phase_sum = running(spec_phase)
    offsets = jnp.zeros((1, rays), F32)
    for i in range(site_ref.shape[1]):
        offsets = offsets + jnp.where(ray_ref[...] == i, site_ref[0, i], 0.0)

    wait_bytes(in_total, n - 1, total_sem)
    sources = in_total[...]
    before = jnp.sum(jnp.where(iota(sources.shape, 0) < me, sources, 0.0), axis=0)
    step_len = 4.0 / (n * gates)
    refl_ref[...] = log_refl - 2.0 * step_len * (before[0:1] + atten_depth)
    phase_ref[...] = 2.0 * step_len * (before[1:2] + phase_sum) + offsets

    wait_bytes(in_total, n - 1, send_sem.at[2])


def finish(refl_ref, phase_ref, refl_out, phase_out):
    refl_out[...] = refl_ref[...]
    phase_out[...] = phase_ref[...]


def local(mass, classes, routes, beam_weight, vertical_weight, ray_site, fit_table, site_phase):
    n = lax.axis_size("rng")
    blocks, cols, levels = mass.shape
    gates, rays, slot_cols = beam_weight.shape
    cap = slot_cols // (n * cols)
    cells = gates * rays
    chunk = cap * cols
    vmem, hbm = pl.BlockSpec(memory_space=pltpu.VMEM), pl.BlockSpec(memory_space=pl.ANY)
    refl, phase = pl.pallas_call(
        functools.partial(kernel, n, cap),
        out_shape=(jax.ShapeDtypeStruct((gates, rays), F32),) * 2,
        in_specs=[hbm] * 8,
        out_specs=(vmem, vmem),
        scratch_shapes=[
            pltpu.VMEM(mass.shape, BF16),
            pltpu.VMEM(classes.shape[::-1], jnp.int32),
            pltpu.VMEM(routes.shape[::-1], jnp.int32),
            pltpu.VMEM((1, rays), jnp.int32),
            pltpu.VMEM(fit_table.shape[::-1], F32),
            pltpu.SMEM((1, site_phase.shape[0]), F32),
            pltpu.VMEM((PLANES, cells, slot_cols // PLANES), BF16),
            pltpu.VMEM((cells, levels), BF16),
            pltpu.VMEM((levels, cells), F32),
            pltpu.VMEM((blocks * cols, levels), F32),
            pltpu.VMEM((slot_cols, levels), F32),
            pltpu.VMEM((n, chunk, levels), BF16),
            pltpu.VMEM((n, 1, 128), F32),
            pltpu.VMEM((n, chunk, levels), BF16),
            pltpu.VMEM((n, 1, 128), F32),
            pltpu.VMEM((2, rays), F32),
            pltpu.VMEM((n, 2, rays), F32),
            pltpu.VMEM((3, 8, cells), F32),
            pltpu.SemaphoreType.DMA((PLANES + 7,)),
            pltpu.SemaphoreType.DMA((3,)),
            pltpu.SemaphoreType.DMA((PLANES,)),
            pltpu.SemaphoreType.DMA((PLANES,)),
            pltpu.SemaphoreType.DMA,
        ],
        compiler_params=pltpu.CompilerParams(
            collective_id=0, has_side_effects=True, vmem_limit_bytes=56 * 1024 * 1024
        ),
    )(
        mass, classes.T, routes.T, ray_site.reshape(1, rays), fit_table.T, site_phase.reshape(1, -1),
        beam_weight.reshape(cells, slot_cols), vertical_weight.reshape(cells, levels),
    )
    return pl.pallas_call(
        finish,
        out_shape=(jax.ShapeDtypeStruct((gates, rays), F32),) * 2,
        in_specs=[vmem, vmem],
        out_specs=(vmem, vmem),
    )(refl, phase)


def solution(mesh):
    placed = (
        P(("grp", "rng"), None, None),
        P(("grp", "rng"), None),
        P(("grp", "rng"), None),
        P(("grp", "rng"), None, None),
        P(("grp", "rng"), None, None),
        P("grp"),
        P(),
        P("grp"),
    )
    return jax.shard_map(
        local,
        mesh=mesh,
        in_specs=placed,
        out_specs=(P(("grp", "rng"), None), P(("grp", "rng"), None)),
        check_vma=False,
    )
```

```python
import functools

import jax
import jax.numpy as jnp
from jax import lax
from jax.experimental import pallas as pl
from jax.experimental.pallas import tpu as pltpu
from jax.sharding import PartitionSpec as P

MESH = pl.DeviceIdType.MESH
BF16, F32 = jnp.bfloat16, jnp.float32
PLANES = 4


def iota(shape, dim):
    return lax.broadcasted_iota(jnp.int32, shape, dim)


def block_of(index, size):
    return jnp.floor((index.astype(F32) + 0.5) * (1.0 / size))


def dot(a, b, contract=((1,), (0,)), precision=None):
    return lax.dot_general(
        a, b, (contract, ((), ())), preferred_element_type=F32, precision=precision
    )


def kernel(
    n, cap,
    mass_hbm, classes_hbm, routes_hbm, ray_hbm, table_hbm, site_hbm, weight_hbm, vertical_hbm,
    refl_ref, phase_ref,
    mass_ref, classes_ref, routes_ref, ray_ref, table_ref, site_ref,
    weight, vertical, vertical_t, mass_f32, slots_f32, out_mass, out_class, in_mass, in_class,
    out_total, in_total, beam_acc, coeff_ref, load_sem, send_sem, mass_sem, class_sem, total_sem,
):
    me = lax.axis_index("rng")
    blocks, cols, levels = mass_ref.shape
    gates, rays = refl_ref.shape
    members = n // PLANES
    chunk = cap * cols
    depth = members * chunk
    slots = n * cap
    plane, place = me // members, me % members
    half = plane // 2

    def to(rank):
        return {"rng": rank}

    barrier = pltpu.get_barrier_semaphore()

    def each(z, start, act):
        def step(i, _):
            act(z * members + (place + i) % members)
            return 0

        lax.fori_loop(start, members, step, 0, unroll=n <= 16)

    near = plane + 1 - 2 * (plane % 2)
    far, last = (plane + 2) % PLANES, PLANES - 1 - plane
    others = ((last, 0), (far, 0), (near, 0), (plane, 1))

    def greet(target):
        pl.semaphore_signal(barrier, 1, device_id=to(target), device_id_type=MESH)

    for z, start in others:
        each(z, start, greet)

    small = [
        pltpu.make_async_copy(source, target, load_sem.at[PLANES + 1 + i])
        for i, (source, target) in enumerate(
            (
                (routes_hbm, routes_ref),
                (mass_hbm, mass_ref),
                (classes_hbm, classes_ref),
                (table_hbm, table_ref),
                (ray_hbm, ray_ref),
                (site_hbm, site_ref),
            )
        )
    ]
    for copy in small:
        copy.start()

    def weight_load(z):
        return pltpu.make_async_copy(
            weight_hbm.at[:, pl.ds(z * depth, depth)], weight.at[z], load_sem.at[z]
        )

    vertical_load = pltpu.make_async_copy(vertical_hbm, vertical, load_sem.at[PLANES])
    vertical_load.start()
    for z in range(PLANES):
        weight_load(z).start()

    for copy in small[:3]:
        copy.wait()

    owner = iota((n, blocks), 0)
    named = (routes_ref[0:1, :] == owner) | (routes_ref[1:2, :] == owner)
    earlier = (iota((blocks, blocks), 0) < iota((blocks, blocks), 1)).astype(F32).astype(BF16)
    position = dot(named.astype(F32).astype(BF16), earlier)
    position = jnp.where(named, position, -1.0).astype(BF16)
    row = iota((slots, n), 0).astype(F32)
    owns = (block_of(row, cap) == iota((slots, n), 1).astype(F32)).astype(F32).astype(BF16)
    row = iota((slots, blocks), 0).astype(F32)
    fills = (dot(owns, position) == row - cap * block_of(row, cap)).astype(F32).astype(BF16)

    mass_f32[...] = mass_ref[...].astype(F32).reshape(blocks * cols, levels)
    by_block = jnp.concatenate(
        [mass_f32[pl.ds(c, blocks, stride=cols), :].astype(BF16) for c in range(cols)], axis=1
    )
    picked = dot(fills, by_block)
    for c in range(cols):
        slots_f32[pl.ds(c, slots, stride=cols), :] = picked[:, c * levels : (c + 1) * levels]
    out_mass[...] = slots_f32[...].astype(BF16).reshape(n, chunk, levels)

    slot_class = dot(fills, classes_ref[...].astype(F32).astype(BF16), ((1,), (1,))).astype(BF16)
    tile = iota((cols, 128), 1).astype(F32)
    tile = tile - cols * block_of(tile, cols) == iota((cols, 128), 0).astype(F32)
    row = iota((slots, 128), 0).astype(F32)
    own_lanes = block_of(iota((slots, 128), 1), cols) == row - cap * block_of(row, cap)
    tiled = jnp.where(own_lanes, dot(slot_class, tile.astype(F32).astype(BF16)), 0.0).astype(BF16)
    spread = (block_of(iota((n, slots), 1), cap) == iota((n, slots), 0).astype(F32))
    class_rows = dot(spread.astype(F32).astype(BF16), tiled)
    out_class[...] = class_rows.reshape(n, 1, 128)

    def mass_copy(target):
        return pltpu.make_async_remote_copy(
            src_ref=out_mass.at[target], dst_ref=in_mass.at[me],
            send_sem=send_sem.at[0], recv_sem=mass_sem.at[plane],
            device_id=to(target), device_id_type=MESH,
        )

    def class_copy(target):
        return pltpu.make_async_remote_copy(
            src_ref=out_class.at[target], dst_ref=in_class.at[me],
            send_sem=send_sem.at[1], recv_sem=class_sem.at[plane],
            device_id=to(target), device_id_type=MESH,
        )

    def total_copy(target):
        return pltpu.make_async_remote_copy(
            src_ref=out_total, dst_ref=in_total.at[me],
            send_sem=send_sem.at[2], recv_sem=total_sem,
            device_id=to(target), device_id_type=MESH,
        )

    def wait_bytes(ref, count, sem):
        part = ref.at[pl.ds(0, count)]
        pltpu.make_async_copy(part, part, sem).wait()

    pl.semaphore_wait(barrier, n - 1)
    order = ((far, 0), (last, 0), (near, 0), (plane, 1))
    for z, start in order:
        each(z, start, lambda target: class_copy(target).start())
    for z, start in order:
        each(z, start, lambda target: mass_copy(target).start())

    in_mass[me] = out_mass[me]
    in_class[me] = out_class[me]

    for copy in small[3:]:
        copy.wait()
    vertical_load.wait()
    vertical_t[...] = vertical[...].astype(F32).T
    for z in range(PLANES):
        weight_load(z).wait()

    lane = iota((chunk, depth), 1)
    lane_place = block_of(lane, chunk)
    unroll = (lane.astype(F32) - chunk * lane_place == iota((chunk, depth), 0).astype(F32))
    unroll = unroll.astype(F32).astype(BF16)
    from_place = block_of(iota((members, depth), 1), chunk) == iota((members, depth), 0).astype(F32)

    def fits_of(z):
        class_grid = in_class[pl.ds(z * members, members)].reshape(members, 128)[:, :chunk]
        class_row = dot(class_grid.astype(BF16), unroll)
        class_row = jnp.sum(jnp.where(from_place, class_row, 0.0), axis=0, keepdims=True)
        onehot = (class_row == iota((table_ref.shape[1], depth), 0).astype(F32)).astype(F32)
        coeff_ref[z] = dot(table_ref[...], onehot, precision=lax.Precision.HIGHEST)

    def absorb(z, initial):
        coeffs = coeff_ref[z]
        mass_t = in_mass[pl.ds(z * members, members)].reshape(depth, levels).astype(F32).T
        positive = mass_t > 0
        log_mass = jnp.log2(jnp.where(positive, mass_t, 1.0))
        fields_t = jnp.concatenate(
            [
                jnp.where(
                    positive,
                    coeffs[2 * j : 2 * j + 1] * jnp.exp2(coeffs[2 * j + 1 : 2 * j + 2] * log_mass),
                    0.0,
                ).astype(BF16)
                for j in range(3)
            ],
            axis=0,
        )
        for g in range(gates):
            cells = slice(g * rays, (g + 1) * rays)
            sampled = dot(fields_t, weight[z, cells, :], ((1,), (1,)))
            v = vertical_t[:, cells]
            for j in range(3):
                part = sampled[j * levels : (j + 1) * levels] * v
                part = jnp.sum(part.reshape(levels // 8, 8, rays), axis=0)
                if initial:
                    beam_acc[j, :, cells] = part
                else:
                    beam_acc[j, :, cells] += part

    wait_bytes(in_class, members - 1, class_sem.at[plane])
    for z in (near, far, last):
        wait_bytes(in_class, members, class_sem.at[z])
    for z in range(PLANES):
        fits_of(z)
    wait_bytes(in_mass, members - 1, mass_sem.at[plane])
    absorb(plane, True)
    for z in (near, far, last):
        wait_bytes(in_mass, members, mass_sem.at[z])
        absorb(z, False)

    gate_row = iota((gates, rays), 0)

    def gate_rows(j):
        rows = jnp.zeros((gates, rays), F32)
        for g in range(gates):
            beam = jnp.sum(beam_acc[j, :, g * rays : (g + 1) * rays], axis=0, keepdims=True)
            rows = jnp.where(gate_row == g, beam, rows)
        return rows

    for j in range(2):
        sums = beam_acc[j + 1, :, 0:rays]
        for g in range(1, gates):
            sums = sums + beam_acc[j + 1, :, g * rays : (g + 1) * rays]
        out_total[j : j + 1, :] = jnp.sum(sums, axis=0, keepdims=True)
    for z, start in others:
        each(z, start, lambda target: total_copy(target).start())

    atten, spec_phase = gate_rows(1), gate_rows(2)
    in_total[me] = out_total[...]
    wait_bytes(out_mass, n - 1, send_sem.at[0])
    wait_bytes(out_class, n - 1, send_sem.at[1])

    def running(rows):
        sums = jnp.zeros((gates, rays), F32)
        for g in range(gates):
            sums = sums + jnp.where(gate_row >= g, rows[g : g + 1], 0.0)
        return sums

    log_refl = jnp.log(gate_rows(0))
    atten_depth = running(atten) - 0.5 * atten
    phase_sum = running(spec_phase)
    offsets = jnp.zeros((1, rays), F32)
    for i in range(site_ref.shape[1]):
        offsets = offsets + jnp.where(ray_ref[...] == i, site_ref[0, i], 0.0)

    wait_bytes(in_total, n - 1, total_sem)
    sources = in_total[...]
    before = jnp.sum(jnp.where(iota(sources.shape, 0) < me, sources, 0.0), axis=0)
    step_len = 4.0 / (n * gates)
    refl_ref[...] = log_refl - 2.0 * step_len * (before[0:1] + atten_depth)
    phase_ref[...] = 2.0 * step_len * (before[1:2] + phase_sum) + offsets

    wait_bytes(in_total, n - 1, send_sem.at[2])


def finish(refl_ref, phase_ref, refl_out, phase_out):
    refl_out[...] = refl_ref[...]
    phase_out[...] = phase_ref[...]


def local(mass, classes, routes, beam_weight, vertical_weight, ray_site, fit_table, site_phase):
    n = lax.axis_size("rng")
    blocks, cols, levels = mass.shape
    gates, rays, slot_cols = beam_weight.shape
    cap = slot_cols // (n * cols)
    cells = gates * rays
    chunk = cap * cols
    vmem, hbm = pl.BlockSpec(memory_space=pltpu.VMEM), pl.BlockSpec(memory_space=pl.ANY)
    refl, phase = pl.pallas_call(
        functools.partial(kernel, n, cap),
        out_shape=(jax.ShapeDtypeStruct((gates, rays), F32),) * 2,
        in_specs=[hbm] * 8,
        out_specs=(vmem, vmem),
        scratch_shapes=[
            pltpu.VMEM(mass.shape, BF16),
            pltpu.VMEM(classes.shape[::-1], jnp.int32),
            pltpu.VMEM(routes.shape[::-1], jnp.int32),
            pltpu.VMEM((1, rays), jnp.int32),
            pltpu.VMEM(fit_table.shape[::-1], F32),
            pltpu.SMEM((1, site_phase.shape[0]), F32),
            pltpu.VMEM((PLANES, cells, slot_cols // PLANES), BF16),
            pltpu.VMEM((cells, levels), BF16),
            pltpu.VMEM((levels, cells), F32),
            pltpu.VMEM((blocks * cols, levels), F32),
            pltpu.VMEM((slot_cols, levels), F32),
            pltpu.VMEM((n, chunk, levels), BF16),
            pltpu.VMEM((n, 1, 128), F32),
            pltpu.VMEM((n, chunk, levels), BF16),
            pltpu.VMEM((n, 1, 128), F32),
            pltpu.VMEM((2, rays), F32),
            pltpu.VMEM((n, 2, rays), F32),
            pltpu.VMEM((3, 8, cells), F32),
            pltpu.VMEM((PLANES, fit_table.shape[1], slot_cols // PLANES), F32),
            pltpu.SemaphoreType.DMA((PLANES + 7,)),
            pltpu.SemaphoreType.DMA((3,)),
            pltpu.SemaphoreType.DMA((PLANES,)),
            pltpu.SemaphoreType.DMA((PLANES,)),
            pltpu.SemaphoreType.DMA,
        ],
        compiler_params=pltpu.CompilerParams(
            collective_id=0, has_side_effects=True, vmem_limit_bytes=56 * 1024 * 1024
        ),
    )(
        mass, classes.T, routes.T, ray_site.reshape(1, rays), fit_table.T, site_phase.reshape(1, -1),
        beam_weight.reshape(cells, slot_cols), vertical_weight.reshape(cells, levels),
    )
    return pl.pallas_call(
        finish,
        out_shape=(jax.ShapeDtypeStruct((gates, rays), F32),) * 2,
        in_specs=[vmem, vmem],
        out_specs=(vmem, vmem),
    )(refl, phase)


def solution(mesh):
    placed = (
        P(("grp", "rng"), None, None),
        P(("grp", "rng"), None),
        P(("grp", "rng"), None),
        P(("grp", "rng"), None, None),
        P(("grp", "rng"), None, None),
        P("grp"),
        P(),
        P("grp"),
    )
    return jax.shard_map(
        local,
        mesh=mesh,
        in_specs=placed,
        out_specs=(P(("grp", "rng"), None), P(("grp", "rng"), None)),
        check_vma=False,
    )
```

```python
import functools

import jax
import jax.numpy as jnp
from jax import lax
from jax.experimental import pallas as pl
from jax.experimental.pallas import tpu as pltpu
from jax.sharding import PartitionSpec as P

MESH = pl.DeviceIdType.MESH
BF16, F32 = jnp.bfloat16, jnp.float32
PLANES = 4


def iota(shape, dim):
    return lax.broadcasted_iota(jnp.int32, shape, dim)


def block_of(index, size):
    return jnp.floor((index.astype(F32) + 0.5) * (1.0 / size))


def dot(a, b, contract=((1,), (0,)), precision=None):
    return lax.dot_general(
        a, b, (contract, ((), ())), preferred_element_type=F32, precision=precision
    )


def kernel(
    n, cap,
    mass_hbm, classes_hbm, routes_hbm, ray_hbm, table_hbm, site_hbm, weight_hbm, vertical_hbm,
    refl_ref, phase_ref,
    mass_ref, classes_ref, routes_ref, ray_ref, table_ref, site_ref,
    weight, vertical, vertical_t, mass_f32, slots_f32, out_mass, out_class, in_mass, in_class,
    out_total, in_total, beam_acc, coeff_ref, load_sem, send_sem, mass_sem, class_sem, total_sem,
):
    me = lax.axis_index("rng")
    blocks, cols, levels = mass_ref.shape
    gates, rays = refl_ref.shape
    members = n // PLANES
    chunk = cap * cols
    depth = members * chunk
    slots = n * cap
    plane, place = me // members, me % members
    half = plane // 2

    def to(rank):
        return {"rng": rank}

    barrier = pltpu.get_barrier_semaphore()

    def each(z, start, act):
        def step(i, _):
            act(z * members + (place + i) % members)
            return 0

        lax.fori_loop(start, members, step, 0, unroll=n <= 16)

    near = plane + 1 - 2 * (plane % 2)
    far, last = (plane + 2) % PLANES, PLANES - 1 - plane
    others = ((last, 0), (far, 0), (near, 0), (plane, 1))

    def greet(target):
        pl.semaphore_signal(barrier, 1, device_id=to(target), device_id_type=MESH)

    for z, start in others:
        each(z, start, greet)

    small = [
        pltpu.make_async_copy(source, target, load_sem.at[PLANES + 1 + i])
        for i, (source, target) in enumerate(
            (
                (routes_hbm, routes_ref),
                (mass_hbm, mass_ref),
                (classes_hbm, classes_ref),
                (table_hbm, table_ref),
                (ray_hbm, ray_ref),
                (site_hbm, site_ref),
            )
        )
    ]
    for copy in small:
        copy.start()

    def weight_load(z):
        return pltpu.make_async_copy(
            weight_hbm.at[:, pl.ds(z * depth, depth)], weight.at[z], load_sem.at[z]
        )

    vertical_load = pltpu.make_async_copy(vertical_hbm, vertical, load_sem.at[PLANES])
    vertical_load.start()
    for z in range(PLANES):
        weight_load(z).start()

    for copy in small[:3]:
        copy.wait()

    owner = iota((n, blocks), 0)
    named = (routes_ref[0:1, :] == owner) | (routes_ref[1:2, :] == owner)
    earlier = (iota((blocks, blocks), 0) < iota((blocks, blocks), 1)).astype(F32).astype(BF16)
    position = dot(named.astype(F32).astype(BF16), earlier)
    position = jnp.where(named, position, -1.0).astype(BF16)
    row = iota((slots, n), 0).astype(F32)
    owns = (block_of(row, cap) == iota((slots, n), 1).astype(F32)).astype(F32).astype(BF16)
    row = iota((slots, blocks), 0).astype(F32)
    fills = (dot(owns, position) == row - cap * block_of(row, cap)).astype(F32).astype(BF16)

    mass_f32[...] = mass_ref[...].astype(F32).reshape(blocks * cols, levels)
    by_block = jnp.concatenate(
        [mass_f32[pl.ds(c, blocks, stride=cols), :].astype(BF16) for c in range(cols)], axis=1
    )
    picked = dot(fills, by_block)
    for c in range(cols):
        slots_f32[pl.ds(c, slots, stride=cols), :] = picked[:, c * levels : (c + 1) * levels]
    out_mass[...] = slots_f32[...].astype(BF16).reshape(n, chunk, levels)

    slot_class = dot(fills, classes_ref[...].astype(F32).astype(BF16), ((1,), (1,))).astype(BF16)
    tile = iota((cols, 128), 1).astype(F32)
    tile = tile - cols * block_of(tile, cols) == iota((cols, 128), 0).astype(F32)
    row = iota((slots, 128), 0).astype(F32)
    own_lanes = block_of(iota((slots, 128), 1), cols) == row - cap * block_of(row, cap)
    tiled = jnp.where(own_lanes, dot(slot_class, tile.astype(F32).astype(BF16)), 0.0).astype(BF16)
    spread = (block_of(iota((n, slots), 1), cap) == iota((n, slots), 0).astype(F32))
    class_rows = dot(spread.astype(F32).astype(BF16), tiled)
    out_class[...] = class_rows.reshape(n, 1, 128)

    def mass_copy(target):
        return pltpu.make_async_remote_copy(
            src_ref=out_mass.at[target], dst_ref=in_mass.at[me],
            send_sem=send_sem.at[0], recv_sem=mass_sem.at[plane],
            device_id=to(target), device_id_type=MESH,
        )

    def class_copy(target):
        return pltpu.make_async_remote_copy(
            src_ref=out_class.at[target], dst_ref=in_class.at[me],
            send_sem=send_sem.at[1], recv_sem=class_sem.at[plane],
            device_id=to(target), device_id_type=MESH,
        )

    def total_copy(target, distance):
        return pltpu.make_async_remote_copy(
            src_ref=out_total, dst_ref=in_total.at[me],
            send_sem=send_sem.at[2 + distance], recv_sem=total_sem.at[plane],
            device_id=to(target), device_id_type=MESH,
        )

    def wait_bytes(ref, count, sem):
        part = ref.at[pl.ds(0, count)]
        pltpu.make_async_copy(part, part, sem).wait()

    pl.semaphore_wait(barrier, n - 1)
    order = ((far, 0), (last, 0), (near, 0), (plane, 1))
    for z, start in order:
        each(z, start, lambda target: class_copy(target).start())
    for z, start in order:
        each(z, start, lambda target: mass_copy(target).start())

    in_mass[me] = out_mass[me]
    in_class[me] = out_class[me]

    for copy in small[3:]:
        copy.wait()
    vertical_load.wait()
    vertical_t[...] = vertical[...].astype(F32).T
    for z in range(PLANES):
        weight_load(z).wait()

    lane = iota((chunk, depth), 1)
    lane_place = block_of(lane, chunk)
    unroll = (lane.astype(F32) - chunk * lane_place == iota((chunk, depth), 0).astype(F32))
    unroll = unroll.astype(F32).astype(BF16)
    from_place = block_of(iota((members, depth), 1), chunk) == iota((members, depth), 0).astype(F32)

    def fits_of(z):
        class_grid = in_class[pl.ds(z * members, members)].reshape(members, 128)[:, :chunk]
        class_row = dot(class_grid.astype(BF16), unroll)
        class_row = jnp.sum(jnp.where(from_place, class_row, 0.0), axis=0, keepdims=True)
        onehot = (class_row == iota((table_ref.shape[1], depth), 0).astype(F32)).astype(F32)
        coeff_ref[z] = dot(table_ref[...], onehot, precision=lax.Precision.HIGHEST)

    def absorb(z, initial):
        coeffs = coeff_ref[z]
        mass_t = in_mass[pl.ds(z * members, members)].reshape(depth, levels).astype(F32).T
        positive = mass_t > 0
        log_mass = jnp.log2(jnp.where(positive, mass_t, 1.0))
        fields_t = jnp.concatenate(
            [
                jnp.where(
                    positive,
                    coeffs[2 * j : 2 * j + 1] * jnp.exp2(coeffs[2 * j + 1 : 2 * j + 2] * log_mass),
                    0.0,
                ).astype(BF16)
                for j in range(3)
            ],
            axis=0,
        )
        for g in range(gates):
            cells = slice(g * rays, (g + 1) * rays)
            sampled = dot(fields_t, weight[z, cells, :], ((1,), (1,)))
            v = vertical_t[:, cells]
            for j in range(3):
                part = sampled[j * levels : (j + 1) * levels] * v
                part = jnp.sum(part.reshape(levels // 8, 8, rays), axis=0)
                if initial:
                    beam_acc[j, :, cells] = part
                else:
                    beam_acc[j, :, cells] += part

    wait_bytes(in_class, members - 1, class_sem.at[plane])
    for z in (near, far, last):
        wait_bytes(in_class, members, class_sem.at[z])
    for z in range(PLANES):
        fits_of(z)
    wait_bytes(in_mass, members - 1, mass_sem.at[plane])
    absorb(plane, True)
    for z in (near, far, last):
        wait_bytes(in_mass, members, mass_sem.at[z])
        absorb(z, False)

    gate_row = iota((gates, rays), 0)

    def gate_rows(j):
        rows = jnp.zeros((gates, rays), F32)
        for g in range(gates):
            beam = jnp.sum(beam_acc[j, :, g * rays : (g + 1) * rays], axis=0, keepdims=True)
            rows = jnp.where(gate_row == g, beam, rows)
        return rows

    for j in range(2):
        sums = beam_acc[j + 1, :, 0:rays]
        for g in range(1, gates):
            sums = sums + beam_acc[j + 1, :, g * rays : (g + 1) * rays]
        out_total[j : j + 1, :] = jnp.sum(sums, axis=0, keepdims=True)
    for k in range(PLANES - 1, 0, -1):

        @pl.when(plane + k < PLANES)
        def _():
            each(plane + k, 0, lambda target: total_copy(target, k).start())

    each(plane, 1, lambda target: total_copy(target, 0).start())

    atten, spec_phase = gate_rows(1), gate_rows(2)
    in_total[me] = out_total[...]
    wait_bytes(out_mass, n - 1, send_sem.at[0])
    wait_bytes(out_class, n - 1, send_sem.at[1])

    def running(rows):
        sums = jnp.zeros((gates, rays), F32)
        for g in range(gates):
            sums = sums + jnp.where(gate_row >= g, rows[g : g + 1], 0.0)
        return sums

    log_refl = jnp.log(gate_rows(0))
    atten_depth = running(atten) - 0.5 * atten
    phase_sum = running(spec_phase)
    offsets = jnp.zeros((1, rays), F32)
    for i in range(site_ref.shape[1]):
        offsets = offsets + jnp.where(ray_ref[...] == i, site_ref[0, i], 0.0)

    wait_bytes(in_total, members - 1, total_sem.at[plane])
    for k in range(1, PLANES):

        @pl.when(plane - k >= 0)
        def _():
            wait_bytes(in_total, members, total_sem.at[plane - k])

    sources = in_total[...]
    before = jnp.sum(jnp.where(iota(sources.shape, 0) < me, sources, 0.0), axis=0)
    step_len = 4.0 / (n * gates)
    refl_ref[...] = log_refl - 2.0 * step_len * (before[0:1] + atten_depth)
    phase_ref[...] = 2.0 * step_len * (before[1:2] + phase_sum) + offsets

    wait_bytes(in_total, members - 1, send_sem.at[2])
    for k in range(1, PLANES):

        @pl.when(plane + k < PLANES)
        def _():
            wait_bytes(in_total, members, send_sem.at[2 + k])


def finish(refl_ref, phase_ref, refl_out, phase_out):
    refl_out[...] = refl_ref[...]
    phase_out[...] = phase_ref[...]


def local(mass, classes, routes, beam_weight, vertical_weight, ray_site, fit_table, site_phase):
    n = lax.axis_size("rng")
    blocks, cols, levels = mass.shape
    gates, rays, slot_cols = beam_weight.shape
    cap = slot_cols // (n * cols)
    cells = gates * rays
    chunk = cap * cols
    vmem, hbm = pl.BlockSpec(memory_space=pltpu.VMEM), pl.BlockSpec(memory_space=pl.ANY)
    refl, phase = pl.pallas_call(
        functools.partial(kernel, n, cap),
        out_shape=(jax.ShapeDtypeStruct((gates, rays), F32),) * 2,
        in_specs=[hbm] * 8,
        out_specs=(vmem, vmem),
        scratch_shapes=[
            pltpu.VMEM(mass.shape, BF16),
            pltpu.VMEM(classes.shape[::-1], jnp.int32),
            pltpu.VMEM(routes.shape[::-1], jnp.int32),
            pltpu.VMEM((1, rays), jnp.int32),
            pltpu.VMEM(fit_table.shape[::-1], F32),
            pltpu.SMEM((1, site_phase.shape[0]), F32),
            pltpu.VMEM((PLANES, cells, slot_cols // PLANES), BF16),
            pltpu.VMEM((cells, levels), BF16),
            pltpu.VMEM((levels, cells), F32),
            pltpu.VMEM((blocks * cols, levels), F32),
            pltpu.VMEM((slot_cols, levels), F32),
            pltpu.VMEM((n, chunk, levels), BF16),
            pltpu.VMEM((n, 1, 128), F32),
            pltpu.VMEM((n, chunk, levels), BF16),
            pltpu.VMEM((n, 1, 128), F32),
            pltpu.VMEM((2, rays), F32),
            pltpu.VMEM((n, 2, rays), F32),
            pltpu.VMEM((3, 8, cells), F32),
            pltpu.VMEM((PLANES, fit_table.shape[1], slot_cols // PLANES), F32),
            pltpu.SemaphoreType.DMA((PLANES + 7,)),
            pltpu.SemaphoreType.DMA((2 + PLANES,)),
            pltpu.SemaphoreType.DMA((PLANES,)),
            pltpu.SemaphoreType.DMA((PLANES,)),
            pltpu.SemaphoreType.DMA((PLANES,)),
        ],
        compiler_params=pltpu.CompilerParams(
            collective_id=0, has_side_effects=True, vmem_limit_bytes=56 * 1024 * 1024
        ),
    )(
        mass, classes.T, routes.T, ray_site.reshape(1, rays), fit_table.T, site_phase.reshape(1, -1),
        beam_weight.reshape(cells, slot_cols), vertical_weight.reshape(cells, levels),
    )
    return pl.pallas_call(
        finish,
        out_shape=(jax.ShapeDtypeStruct((gates, rays), F32),) * 2,
        in_specs=[vmem, vmem],
        out_specs=(vmem, vmem),
    )(refl, phase)


def solution(mesh):
    placed = (
        P(("grp", "rng"), None, None),
        P(("grp", "rng"), None),
        P(("grp", "rng"), None),
        P(("grp", "rng"), None, None),
        P(("grp", "rng"), None, None),
        P("grp"),
        P(),
        P("grp"),
    )
    return jax.shard_map(
        local,
        mesh=mesh,
        in_specs=placed,
        out_specs=(P(("grp", "rng"), None), P(("grp", "rng"), None)),
        check_vma=False,
    )
```

```python
import functools

import jax
import jax.numpy as jnp
from jax import lax
from jax.experimental import pallas as pl
from jax.experimental.pallas import tpu as pltpu
from jax.sharding import PartitionSpec as P

MESH = pl.DeviceIdType.MESH
BF16, F32 = jnp.bfloat16, jnp.float32
PLANES = 4


def iota(shape, dim):
    return lax.broadcasted_iota(jnp.int32, shape, dim)


def block_of(index, size):
    return jnp.floor((index.astype(F32) + 0.5) * (1.0 / size))


def dot(a, b, contract=((1,), (0,)), precision=None):
    return lax.dot_general(
        a, b, (contract, ((), ())), preferred_element_type=F32, precision=precision
    )


def kernel(
    n, cap,
    mass_hbm, classes_hbm, routes_hbm, ray_hbm, table_hbm, site_hbm, weight_hbm, vertical_hbm,
    refl_ref, phase_ref,
    mass_ref, classes_ref, routes_ref, ray_ref, table_ref, site_ref,
    weight, vertical, vertical_t, mass_f32, slots_f32, out_mass, out_class, in_mass, in_class,
    out_total, in_total, beam_acc, coeff_ref, load_sem, send_sem, mass_sem, class_sem, total_sem,
):
    me = lax.axis_index("rng")
    blocks, cols, levels = mass_ref.shape
    gates, rays = refl_ref.shape
    members = n // PLANES
    chunk = cap * cols
    depth = members * chunk
    slots = n * cap
    plane, place = me // members, me % members
    half = plane // 2

    def to(rank):
        return {"rng": rank}

    barrier = pltpu.get_barrier_semaphore()

    def each(z, start, act):
        def step(i, _):
            act(z * members + (place + i) % members)
            return 0

        lax.fori_loop(start, members, step, 0, unroll=n <= 16)

    near = plane + 1 - 2 * (plane % 2)
    far, last = (plane + 2) % PLANES, PLANES - 1 - plane
    others = ((last, 0), (far, 0), (near, 0), (plane, 1))

    def greet(target):
        pl.semaphore_signal(barrier, 1, device_id=to(target), device_id_type=MESH)

    for z, start in others:
        each(z, start, greet)

    small = [
        pltpu.make_async_copy(source, target, load_sem.at[PLANES + 1 + i])
        for i, (source, target) in enumerate(
            (
                (routes_hbm, routes_ref),
                (mass_hbm, mass_ref),
                (classes_hbm, classes_ref),
                (table_hbm, table_ref),
                (ray_hbm, ray_ref),
                (site_hbm, site_ref),
            )
        )
    ]
    for copy in small:
        copy.start()

    def weight_load(z):
        return pltpu.make_async_copy(
            weight_hbm.at[:, pl.ds(z * depth, depth)], weight.at[z], load_sem.at[z]
        )

    vertical_load = pltpu.make_async_copy(vertical_hbm, vertical, load_sem.at[PLANES])
    vertical_load.start()
    for z in range(PLANES):
        weight_load(z).start()

    for copy in small[:3]:
        copy.wait()

    owner = iota((n, blocks), 0)
    named = (routes_ref[0:1, :] == owner) | (routes_ref[1:2, :] == owner)
    earlier = (iota((blocks, blocks), 0) < iota((blocks, blocks), 1)).astype(F32).astype(BF16)
    position = dot(named.astype(F32).astype(BF16), earlier)
    position = jnp.where(named, position, -1.0).astype(BF16)
    row = iota((slots, n), 0).astype(F32)
    owns = (block_of(row, cap) == iota((slots, n), 1).astype(F32)).astype(F32).astype(BF16)
    row = iota((slots, blocks), 0).astype(F32)
    fills = (dot(owns, position) == row - cap * block_of(row, cap)).astype(F32).astype(BF16)

    mass_f32[...] = mass_ref[...].astype(F32).reshape(blocks * cols, levels)
    by_block = jnp.concatenate(
        [mass_f32[pl.ds(c, blocks, stride=cols), :].astype(BF16) for c in range(cols)], axis=1
    )
    picked = dot(fills, by_block)
    for c in range(cols):
        slots_f32[pl.ds(c, slots, stride=cols), :] = picked[:, c * levels : (c + 1) * levels]
    out_mass[...] = slots_f32[...].astype(BF16).reshape(n, chunk, levels)

    slot_class = dot(fills, classes_ref[...].astype(F32).astype(BF16), ((1,), (1,))).astype(BF16)
    tile = iota((cols, 128), 1).astype(F32)
    tile = tile - cols * block_of(tile, cols) == iota((cols, 128), 0).astype(F32)
    row = iota((slots, 128), 0).astype(F32)
    own_lanes = block_of(iota((slots, 128), 1), cols) == row - cap * block_of(row, cap)
    tiled = jnp.where(own_lanes, dot(slot_class, tile.astype(F32).astype(BF16)), 0.0).astype(BF16)
    spread = (block_of(iota((n, slots), 1), cap) == iota((n, slots), 0).astype(F32))
    class_rows = dot(spread.astype(F32).astype(BF16), tiled)
    out_class[...] = class_rows.reshape(n, 1, 128)

    def mass_copy(target):
        return pltpu.make_async_remote_copy(
            src_ref=out_mass.at[target], dst_ref=in_mass.at[me],
            send_sem=send_sem.at[0], recv_sem=mass_sem.at[plane],
            device_id=to(target), device_id_type=MESH,
        )

    def class_copy(target):
        return pltpu.make_async_remote_copy(
            src_ref=out_class.at[target], dst_ref=in_class.at[me],
            send_sem=send_sem.at[1], recv_sem=class_sem.at[plane],
            device_id=to(target), device_id_type=MESH,
        )

    def total_copy(target, distance):
        return pltpu.make_async_remote_copy(
            src_ref=out_total, dst_ref=in_total.at[me],
            send_sem=send_sem.at[2 + distance], recv_sem=total_sem.at[plane],
            device_id=to(target), device_id_type=MESH,
        )

    def wait_bytes(ref, count, sem):
        part = ref.at[pl.ds(0, count)]
        pltpu.make_async_copy(part, part, sem).wait()

    pl.semaphore_wait(barrier, n - 1)
    low = 2 - 2 * half
    order = ((low, 0), (low + 1, 0), (near, 0), (plane, 1))
    for z, start in order:
        each(z, start, lambda target: class_copy(target).start())
    for z, start in order:
        each(z, start, lambda target: mass_copy(target).start())

    in_mass[me] = out_mass[me]
    in_class[me] = out_class[me]

    for copy in small[3:]:
        copy.wait()
    vertical_load.wait()
    vertical_t[...] = vertical[...].astype(F32).T
    for z in range(PLANES):
        weight_load(z).wait()

    lane = iota((chunk, depth), 1)
    lane_place = block_of(lane, chunk)
    unroll = (lane.astype(F32) - chunk * lane_place == iota((chunk, depth), 0).astype(F32))
    unroll = unroll.astype(F32).astype(BF16)
    from_place = block_of(iota((members, depth), 1), chunk) == iota((members, depth), 0).astype(F32)

    def fits_of(z):
        class_grid = in_class[pl.ds(z * members, members)].reshape(members, 128)[:, :chunk]
        class_row = dot(class_grid.astype(BF16), unroll)
        class_row = jnp.sum(jnp.where(from_place, class_row, 0.0), axis=0, keepdims=True)
        onehot = (class_row == iota((table_ref.shape[1], depth), 0).astype(F32)).astype(F32)
        coeff_ref[z] = dot(table_ref[...], onehot, precision=lax.Precision.HIGHEST)

    def absorb(z, initial):
        coeffs = coeff_ref[z]
        mass_t = in_mass[pl.ds(z * members, members)].reshape(depth, levels).astype(F32).T
        positive = mass_t > 0
        log_mass = jnp.log2(jnp.where(positive, mass_t, 1.0))
        fields_t = jnp.concatenate(
            [
                jnp.where(
                    positive,
                    coeffs[2 * j : 2 * j + 1] * jnp.exp2(coeffs[2 * j + 1 : 2 * j + 2] * log_mass),
                    0.0,
                ).astype(BF16)
                for j in range(3)
            ],
            axis=0,
        )
        for g in range(gates):
            cells = slice(g * rays, (g + 1) * rays)
            sampled = dot(fields_t, weight[z, cells, :], ((1,), (1,)))
            v = vertical_t[:, cells]
            for j in range(3):
                part = sampled[j * levels : (j + 1) * levels] * v
                part = jnp.sum(part.reshape(levels // 8, 8, rays), axis=0)
                if initial:
                    beam_acc[j, :, cells] = part
                else:
                    beam_acc[j, :, cells] += part

    wait_bytes(in_class, members - 1, class_sem.at[plane])
    for z in (near, far, last):
        wait_bytes(in_class, members, class_sem.at[z])
    for z in range(PLANES):
        fits_of(z)
    wait_bytes(in_mass, members - 1, mass_sem.at[plane])
    absorb(plane, True)
    for z in (near, 2 - half, 3 - 3 * half):
        wait_bytes(in_mass, members, mass_sem.at[z])
        absorb(z, False)

    gate_row = iota((gates, rays), 0)

    def gate_rows(j):
        rows = jnp.zeros((gates, rays), F32)
        for g in range(gates):
            beam = jnp.sum(beam_acc[j, :, g * rays : (g + 1) * rays], axis=0, keepdims=True)
            rows = jnp.where(gate_row == g, beam, rows)
        return rows

    for j in range(2):
        sums = beam_acc[j + 1, :, 0:rays]
        for g in range(1, gates):
            sums = sums + beam_acc[j + 1, :, g * rays : (g + 1) * rays]
        out_total[j : j + 1, :] = jnp.sum(sums, axis=0, keepdims=True)
    for k in range(PLANES - 1, 0, -1):

        @pl.when(plane + k < PLANES)
        def _():
            each(plane + k, 0, lambda target: total_copy(target, k).start())

    each(plane, 1, lambda target: total_copy(target, 0).start())

    atten, spec_phase = gate_rows(1), gate_rows(2)
    in_total[me] = out_total[...]
    wait_bytes(out_mass, n - 1, send_sem.at[0])
    wait_bytes(out_class, n - 1, send_sem.at[1])

    def running(rows):
        sums = jnp.zeros((gates, rays), F32)
        for g in range(gates):
            sums = sums + jnp.where(gate_row >= g, rows[g : g + 1], 0.0)
        return sums

    log_refl = jnp.log(gate_rows(0))
    atten_depth = running(atten) - 0.5 * atten
    phase_sum = running(spec_phase)
    offsets = jnp.zeros((1, rays), F32)
    for i in range(site_ref.shape[1]):
        offsets = offsets + jnp.where(ray_ref[...] == i, site_ref[0, i], 0.0)

    wait_bytes(in_total, members - 1, total_sem.at[plane])
    for k in range(1, PLANES):

        @pl.when(plane - k >= 0)
        def _():
            wait_bytes(in_total, members, total_sem.at[plane - k])

    sources = in_total[...]
    before = jnp.sum(jnp.where(iota(sources.shape, 0) < me, sources, 0.0), axis=0)
    step_len = 4.0 / (n * gates)
    refl_ref[...] = log_refl - 2.0 * step_len * (before[0:1] + atten_depth)
    phase_ref[...] = 2.0 * step_len * (before[1:2] + phase_sum) + offsets

    wait_bytes(in_total, members - 1, send_sem.at[2])
    for k in range(1, PLANES):

        @pl.when(plane + k < PLANES)
        def _():
            wait_bytes(in_total, members, send_sem.at[2 + k])


def finish(refl_ref, phase_ref, refl_out, phase_out):
    refl_out[...] = refl_ref[...]
    phase_out[...] = phase_ref[...]


def local(mass, classes, routes, beam_weight, vertical_weight, ray_site, fit_table, site_phase):
    n = lax.axis_size("rng")
    blocks, cols, levels = mass.shape
    gates, rays, slot_cols = beam_weight.shape
    cap = slot_cols // (n * cols)
    cells = gates * rays
    chunk = cap * cols
    vmem, hbm = pl.BlockSpec(memory_space=pltpu.VMEM), pl.BlockSpec(memory_space=pl.ANY)
    refl, phase = pl.pallas_call(
        functools.partial(kernel, n, cap),
        out_shape=(jax.ShapeDtypeStruct((gates, rays), F32),) * 2,
        in_specs=[hbm] * 8,
        out_specs=(vmem, vmem),
        scratch_shapes=[
            pltpu.VMEM(mass.shape, BF16),
            pltpu.VMEM(classes.shape[::-1], jnp.int32),
            pltpu.VMEM(routes.shape[::-1], jnp.int32),
            pltpu.VMEM((1, rays), jnp.int32),
            pltpu.VMEM(fit_table.shape[::-1], F32),
            pltpu.SMEM((1, site_phase.shape[0]), F32),
            pltpu.VMEM((PLANES, cells, slot_cols // PLANES), BF16),
            pltpu.VMEM((cells, levels), BF16),
            pltpu.VMEM((levels, cells), F32),
            pltpu.VMEM((blocks * cols, levels), F32),
            pltpu.VMEM((slot_cols, levels), F32),
            pltpu.VMEM((n, chunk, levels), BF16),
            pltpu.VMEM((n, 1, 128), F32),
            pltpu.VMEM((n, chunk, levels), BF16),
            pltpu.VMEM((n, 1, 128), F32),
            pltpu.VMEM((2, rays), F32),
            pltpu.VMEM((n, 2, rays), F32),
            pltpu.VMEM((3, 8, cells), F32),
            pltpu.VMEM((PLANES, fit_table.shape[1], slot_cols // PLANES), F32),
            pltpu.SemaphoreType.DMA((PLANES + 7,)),
            pltpu.SemaphoreType.DMA((2 + PLANES,)),
            pltpu.SemaphoreType.DMA((PLANES,)),
            pltpu.SemaphoreType.DMA((PLANES,)),
            pltpu.SemaphoreType.DMA((PLANES,)),
        ],
        compiler_params=pltpu.CompilerParams(
            collective_id=0, has_side_effects=True, vmem_limit_bytes=56 * 1024 * 1024
        ),
    )(
        mass, classes.T, routes.T, ray_site.reshape(1, rays), fit_table.T, site_phase.reshape(1, -1),
        beam_weight.reshape(cells, slot_cols), vertical_weight.reshape(cells, levels),
    )
    return pl.pallas_call(
        finish,
        out_shape=(jax.ShapeDtypeStruct((gates, rays), F32),) * 2,
        in_specs=[vmem, vmem],
        out_specs=(vmem, vmem),
    )(refl, phase)


def solution(mesh):
    placed = (
        P(("grp", "rng"), None, None),
        P(("grp", "rng"), None),
        P(("grp", "rng"), None),
        P(("grp", "rng"), None, None),
        P(("grp", "rng"), None, None),
        P("grp"),
        P(),
        P("grp"),
    )
    return jax.shard_map(
        local,
        mesh=mesh,
        in_specs=placed,
        out_specs=(P(("grp", "rng"), None), P(("grp", "rng"), None)),
        check_vma=False,
    )
```
